32 devices in a mesh: ctx: 8 (over y, x, core), tp: 4 (over z).
Axes of the slice: x: 2, y: 2, z: 4, core: 2. Of those that a mesh axis runs over, the one named last changes fastest.
Arguments:
- queries: bfloat16 [128, 8192], P('ctx', 'tp'), may hold values from -60 to 60
- rotated_keys: bfloat16 [1024, 1024], P('ctx', 'tp'), may hold values from -7 to 7
- value_rows: bfloat16 [1024, 1024], P('ctx', 'tp'), may hold values from -6 to 6
- span_order: int32 [16], replicated, may hold values from 0 to 15, each once
- targets: int32 [128], replicated, may hold values from 0 to 65535
- out_weight: bfloat16 [8192, 4, 8, 256], P('tp', None, 'ctx'), may hold values from -0.0625 to 0.0625
- residual: bfloat16 [128, 4, 8, 256], P(None, 'tp', 'ctx'), may hold values from -3 to 3
- norm_gain: float32 [4, 8, 256], P('tp', 'ctx'), may hold values from 0.5 to 1.5
- head_weight: bfloat16 [8192, 65536], P('tp', 'ctx'), may hold values from -2.253903 to 2.253903
Outputs:
- loss: float32 [], replicated
- grad_normed: bfloat16 [128, 8192], P('ctx', 'tp')
- grad_head: bfloat16 [8192, 65536], P('tp', 'ctx')
The draws below stay inside these ranges and needn't reach their ends.
Inputs may be any that keep to these rules, and one draw needn't show every extreme that they name: `span_order`: each span number appears once.
All inputs are finite; a program needn't handle non-finite values.
Results may differ from the reference program's by a relative error of at most 0.012.
Values may be sent and summed in bfloat16 or wider, within the bound.
A program may use at most 128 MiB of HBM per device.

```python
import math
import jax
import jax.numpy as jnp
import numpy as np
from jax import lax

D = 8192
QUERY_HEADS = 64
KEY_VALUE_HEADS = 8
HEAD_SIZE = 128
VOCAB = 65536
SPAN = 64
Q_SPAN = 8
SEQUENCE_TOKENS = 1024
QUERY_TOKENS = 128
NSPANS = 16
SLICE = 256
N_CTX = 8
N_TP = 4


def paired_states(key):
    base_key = jax.random.fold_in(key, 907)
    key_layout = (SEQUENCE_TOKENS, KEY_VALUE_HEADS * HEAD_SIZE)
    query_layout = (QUERY_TOKENS, QUERY_HEADS * HEAD_SIZE)
    key_vals = jnp.clip(jax.random.normal(jax.random.fold_in(base_key, 1), key_layout, jnp.float32), -6.0, 6.0)
    query_vals = jnp.clip(jax.random.normal(jax.random.fold_in(base_key, 2), query_layout, jnp.float32), -6.0, 6.0)
    return (query_vals, key_vals)


def draw_queries(key, part):
    return paired_states(key)[0].astype(jnp.bfloat16)


def draw_rotated_keys(key, part):
    return paired_states(key)[1].astype(jnp.bfloat16)


def draw_head_weight(key, part):
    spread = 3.0 * D ** (-0.5)
    normal_vals = jnp.clip(jax.random.normal(jax.random.fold_in(key, 11), (D, VOCAB), jnp.float32), -6.0, 6.0)
    return (normal_vals * spread).astype(jnp.bfloat16)


def touch_ends(entries, stream_key, low, largest):
    spot = [jax.random.randint(jax.random.fold_in(stream_key, axis), (), 0, length) for axis, length in enumerate(entries.shape)]
    widest = entries.shape.index(max(entries.shape))
    next_to = spot[:widest] + [(spot[widest] + 1) % entries.shape[widest]] + spot[widest + 1:]
    return entries.at[tuple(spot)].set(low).at[tuple(next_to)].set(largest)


def levels(key, dims, cuts, smallest, high):
    level, own = 1.0, jax.random.fold_in(key, 6)
    for dim, parts in cuts:
        steps = jnp.exp(jax.random.uniform(jax.random.fold_in(own, dim), (parts,), jnp.float32, smallest / len(cuts), high / len(cuts)))
        level = level * jnp.repeat(steps, dims[dim] // parts).reshape([-1 if axis == dim else 1 for axis in range(len(dims))])
    return level


def cumulative_ranks(amount, slope):
    loads = [(1 << 20) // math.isqrt(standing ** slope) + 1 for standing in range(1, amount + 1)]
    deviation = 1 + sum(loads) // (1 << 30)
    return np.cumsum(np.array([max(1, weight // deviation) for weight in loads]))


def ranked(own_key, shape, amount, lean):
    table = cumulative_ranks(amount, lean)
    pick = jax.random.randint(jax.random.fold_in(own_key, 1), shape, 0, int(table[amount - 1]))
    rank = jnp.searchsorted(jnp.asarray(table, jnp.int32), pick, side="right")
    return jax.random.permutation(jax.random.fold_in(own_key, 2), amount)[rank].astype(jnp.int32)


def bell_draw(key, shape, scale, reach, cuts=(), kind=jnp.bfloat16):
    gain = levels(key, shape, cuts, -0.22, 0.18) if cuts else 1.0
    drawn = jax.random.normal(key, shape, jnp.float32) * scale * gain
    return jnp.minimum(jnp.maximum(drawn, -reach), reach).astype(kind)


def setup_inputs(seed: int = 0) -> dict:
    arg_keys = jax.random.split(jax.random.key(seed), 10)
    return {
        "queries": draw_queries(jax.random.fold_in(arg_keys[9], 71), 0),
        "rotated_keys": draw_rotated_keys(jax.random.fold_in(arg_keys[9], 71), 0),
        "value_rows": bell_draw(arg_keys[2], (SEQUENCE_TOKENS, KEY_VALUE_HEADS * HEAD_SIZE), 1.0, 6.0, ((0, 8), (1, 4))),
        "span_order": jax.random.permutation(arg_keys[3], NSPANS).astype(jnp.int32),
        "targets": touch_ends(ranked(arg_keys[4], (QUERY_TOKENS,), VOCAB, 2), jax.random.fold_in(arg_keys[4], 3), 0, VOCAB - 1).astype(jnp.int32),
        "out_weight": bell_draw(arg_keys[5], (QUERY_HEADS * HEAD_SIZE, N_TP, N_CTX, SLICE), (QUERY_HEADS * HEAD_SIZE) ** -0.5, 0.0625, ((0, 4), (2, 8))),
        "residual": bell_draw(arg_keys[6], (QUERY_TOKENS, N_TP, N_CTX, SLICE), 0.5, 3.0, ((1, 4), (2, 8))),
        "norm_gain": jnp.clip(1.0 + 0.1 * jax.random.normal(arg_keys[7], (N_TP, N_CTX, SLICE), jnp.float32), 0.5, 1.5),
        "head_weight": draw_head_weight(jax.random.fold_in(arg_keys[9], 71), 0),
    }


EPSILON = 1e-05
MASKED = -1e+30

def key_positions(span_order):
    slots = jnp.arange(SEQUENCE_TOKENS, dtype=jnp.int32)
    return span_order[slots // SPAN].astype(jnp.int32) * SPAN + slots % SPAN

def query_positions(span_order):
    slots = jnp.arange(QUERY_TOKENS, dtype=jnp.int32)
    return span_order[slots // Q_SPAN].astype(jnp.int32) * SPAN + (SPAN - Q_SPAN) + slots % Q_SPAN

def reference(queries, rotated_keys, value_rows, span_order, targets, out_weight, residual, norm_gain, head_weight):
    key_pos = key_positions(span_order)
    query_pos = query_positions(span_order)
    visible = key_pos[None, :] <= query_pos[:, None]
    group_size = QUERY_HEADS // KEY_VALUE_HEADS
    grouped_queries = queries.astype(jnp.float32).reshape(QUERY_TOKENS, KEY_VALUE_HEADS, group_size, HEAD_SIZE).transpose(1, 0, 2, 3)
    divided_keys = rotated_keys.astype(jnp.float32).reshape(SEQUENCE_TOKENS, KEY_VALUE_HEADS, HEAD_SIZE).transpose(1, 0, 2)
    divided_values = value_rows.astype(jnp.float32).reshape(SEQUENCE_TOKENS, KEY_VALUE_HEADS, HEAD_SIZE).transpose(1, 0, 2)

    def one_head(inputs):
        head_q, head_k, head_v = inputs
        scores = jnp.einsum('tgd,sd->gts', head_q, head_k) * HEAD_SIZE ** (-0.5)
        scores = jnp.where(visible[None], scores, MASKED)
        peak = lax.optimization_barrier(jnp.max(scores, axis=-1, keepdims=True))
        expo = jnp.exp(scores - peak)
        weights = (expo / lax.optimization_barrier(jnp.sum(expo, axis=-1, keepdims=True))).astype(jnp.bfloat16)
        weights = lax.optimization_barrier(weights).astype(jnp.float32)
        return jnp.einsum('gts,sd->tgd', weights, head_v).astype(jnp.bfloat16)
    heads_out = lax.map(one_head, (grouped_queries, divided_keys, divided_values))
    attn = heads_out.transpose(1, 0, 2, 3).reshape(QUERY_TOKENS, QUERY_HEADS * HEAD_SIZE)
    projected = jnp.dot(attn, out_weight.reshape(QUERY_HEADS * HEAD_SIZE, D), preferred_element_type=jnp.float32)
    hidden = residual.reshape(QUERY_TOKENS, D).astype(jnp.float32) + projected
    mean_sq = lax.optimization_barrier(jnp.mean(hidden * hidden, axis=1))
    normed = (hidden * lax.rsqrt(mean_sq + EPSILON)[:, None] * norm_gain.reshape(D)).astype(jnp.bfloat16)
    logits = jnp.dot(normed, head_weight, preferred_element_type=jnp.float32)
    peak = lax.optimization_barrier(jnp.max(logits, axis=1))
    lse = peak + jnp.log(lax.optimization_barrier(jnp.sum(jnp.exp(logits - peak[:, None]), axis=1)))
    picked = jnp.take_along_axis(logits, targets[:, None].astype(jnp.int32), axis=1)[:, 0]
    loss = jnp.mean(lse - picked)
    target_hit = jnp.arange(VOCAB, dtype=jnp.int32)[None, :] == targets[:, None]
    grad_logits = (jnp.exp(logits - lse[:, None]) - target_hit.astype(jnp.float32)).astype(jnp.bfloat16)
    grad_normed = jnp.dot(grad_logits, head_weight.T, preferred_element_type=jnp.float32).astype(jnp.bfloat16)
    grad_head = jnp.dot(normed.T, grad_logits, preferred_element_type=jnp.float32).astype(jnp.bfloat16)
    return (loss, grad_normed, grad_head)
```

```python
import functools

import jax
import jax.numpy as jnp
from jax import lax
from jax.experimental import pallas as pl
from jax.experimental.pallas import tpu as pltpu
from jax.sharding import PartitionSpec as P

D = 8192
QUERY_HEADS = 64
KEY_VALUE_HEADS = 8
HEAD_SIZE = 128


EPSILON = 1e-05
MASKED = -1e30


def slot_positions(span_order, total_rows, slot_rows, span_rows, first_row):
    slots = jnp.arange(total_rows, dtype=jnp.int32)
    owners = slots // slot_rows
    table = owners[:, None] == jnp.arange(span_order.shape[0], dtype=jnp.int32)[None, :]
    starts = jnp.sum(jnp.where(table, span_order[None, :], 0), axis=1)
    return starts * span_rows + first_row + slots % slot_rows


def head_scores(grouped_queries, piece_keys):
    divided_keys = piece_keys.reshape(piece_keys.shape[0], -1, HEAD_SIZE)
    return jnp.einsum(
        "tkgd,skd->kgts", grouped_queries, divided_keys, preferred_element_type=jnp.float32
    ) * HEAD_SIZE ** (-0.5)


def score_stats(grouped_queries, mine, positions):

    def score_update(carry, piece, offset):
        visible = positions[None, :] <= mine[:, None]

        def score_accumulate(state):
            scores = jnp.where(visible, head_scores(grouped_queries, piece), MASKED)
            fresh = jnp.maximum(state[0], jnp.max(scores, axis=-1))
            added = jnp.sum(jnp.where(visible, jnp.exp(scores - fresh[..., None]), 0.0), axis=-1)
            return (fresh, added)

        return lax.cond(jnp.any(visible), score_accumulate, lambda state: state, carry)

    return score_update


def weighted_values(grouped_queries, mine, positions, peak, totals):

    def weighted_update(carry, pieces, offset):
        piece_keys, piece_values = pieces
        visible = positions[None, :] <= mine[:, None]

        def weighted_accumulate(state):
            scores = jnp.where(visible, head_scores(grouped_queries, piece_keys), MASKED)
            weights = jnp.where(visible, jnp.exp(scores - peak[..., None]), 0.0) / totals[..., None]
            divided_values = piece_values.reshape(piece_values.shape[0], -1, HEAD_SIZE)
            return jnp.einsum(
                "kgts,skd->tkgd",
                weights.astype(jnp.bfloat16),
                divided_values,
                preferred_element_type=jnp.float32,
            )

        return lax.cond(jnp.any(visible), weighted_accumulate, lambda state: state, carry)

    return weighted_update


def per_device(
    queries,
    rotated_keys,
    value_rows,
    span_order,
    targets,
    out_weight,
    residual,
    norm_gain,
    head_weight,
):
    tok_dev = rotated_keys.shape[0]
    q_dev = queries.shape[0]
    span_rows = tok_dev // 2
    q_span = q_dev // 2
    total_keys = tok_dev * lax.axis_size("ctx")
    total_rows = q_dev * lax.axis_size("ctx")
    positions = slot_positions(span_order, total_keys, span_rows, span_rows, 0)
    query_pos = slot_positions(span_order, total_rows, q_span, span_rows, span_rows - q_span)
    mine = lax.dynamic_slice_in_dim(query_pos, lax.axis_index("ctx") * q_dev, q_dev)
    group_size = QUERY_HEADS // KEY_VALUE_HEADS
    local_kv = rotated_keys.shape[1] // HEAD_SIZE
    grouped_queries = queries.reshape(q_dev, local_kv, group_size, HEAD_SIZE)
    start_stats = (
        jnp.full((local_kv, group_size, q_dev), MASKED, jnp.float32),
        jnp.zeros((local_kv, group_size, q_dev), jnp.float32),
    )
    start_acc = jnp.zeros((q_dev, local_kv, group_size, HEAD_SIZE), jnp.float32)
    stats_step = score_stats(grouped_queries, mine, positions)
    all_keys, all_values = (
        lax.all_gather(rotated_keys, "ctx", axis=0, tiled=True),
        lax.all_gather(value_rows, "ctx", axis=0, tiled=True),
    )
    peak, totals = stats_step(start_stats, all_keys, 0)
    value_step = weighted_values(grouped_queries, mine, positions, peak, totals)
    attn_acc = value_step(start_acc, (all_keys, all_values), 0)
    attn = attn_acc.astype(jnp.bfloat16).reshape(q_dev, -1)
    slice_width = out_weight.shape[3]
    out_local = out_weight.reshape(out_weight.shape[0], -1)
    mixed = jnp.dot(
        lax.all_gather(attn, "ctx", axis=0, tiled=True),
        out_local,
        preferred_element_type=jnp.float32,
    )
    mixed = lax.psum_scatter(
        mixed.reshape(total_rows, -1, slice_width), "tp", scatter_dimension=1, tiled=True
    )
    hidden = residual.reshape(total_rows, slice_width).astype(jnp.float32) + mixed.reshape(
        total_rows, slice_width
    )
    squares = lax.psum(jnp.sum(hidden * hidden, axis=1), ("ctx", "tp"))
    normed = (
        hidden * lax.rsqrt(squares / D + EPSILON)[:, None] * norm_gain.reshape(1, slice_width)
    ).astype(jnp.bfloat16)
    block = lax.all_gather(normed, "ctx", axis=1, tiled=True)
    vocab_width = head_weight.shape[1]
    first_col = lax.axis_index("ctx") * vocab_width
    logits = lax.psum_scatter(
        jnp.dot(block, head_weight, preferred_element_type=jnp.float32),
        "tp",
        scatter_dimension=0,
        tiled=True,
    )
    row_targets = lax.dynamic_slice_in_dim(
        targets, lax.axis_index("tp") * logits.shape[0], logits.shape[0]
    )
    columns = jnp.arange(vocab_width, dtype=jnp.int32)[None, :] + first_col
    target_hit = columns == row_targets[:, None]
    local_peak = jnp.max(logits, axis=1)
    picked = jnp.sum(jnp.where(target_hit, logits, 0.0), axis=1)
    row_peak = lax.pmax(local_peak, "ctx")
    expsum = jnp.sum(jnp.exp(logits - row_peak[:, None]), axis=1)
    expsum, picked = lax.psum((expsum, picked), "ctx")
    lse = row_peak + jnp.log(expsum)
    grad_logits = (jnp.exp(logits - lse[:, None]) - target_hit.astype(jnp.float32)).astype(
        jnp.bfloat16
    )
    loss_part = jnp.sum(lse - picked)
    loss = lax.psum(loss_part, "tp") / total_rows
    grad_logits = lax.all_gather(grad_logits, "tp", axis=0, tiled=True)
    grad_normed = lax.psum_scatter(
        lax.dot_general(
            grad_logits, head_weight, (((1,), (1,)), ((), ())), preferred_element_type=jnp.float32
        ),
        "ctx",
        scatter_dimension=0,
        tiled=True,
    ).astype(jnp.bfloat16)
    grad_head = lax.dot_general(
        block, grad_logits, (((0,), (0,)), ((), ())), preferred_element_type=jnp.float32
    ).astype(jnp.bfloat16)
    return (loss, grad_normed, grad_head)


MESH = pl.DeviceIdType.MESH
F32 = jnp.float32
BF16 = jnp.bfloat16


def fused_kernel(
    nc,
    chunk,
    q_ref,
    k_ref,
    v_ref,
    kpos_ref,
    qpos_ref,
    target_ref,
    wo_hbm,
    resid_ref,
    gain_ref,
    w_hbm,
    loss_ref,
    gn_ref,
    block_ref,
    gl_ref,
    w,
    wo,
    kv_all,
    attn,
    mix_out,
    mix_in,
    square_tp,
    square_ctx,
    norm_all,
    part_out,
    pair_in,
    far_in,
    logit,
    pack,
    stat,
    loss_all,
    hidden_grad,
    grad_out,
    grad_in,
    w_sem,
    wo_sem,
    gather_send,
    gather_recv,
    mix_sem,
    square_sem,
    cross_sem,
    part_send,
    part_recv,
    stat_sem,
    loss_sem,
    share_send,
    share_recv,
    grad_sem,
):
    tp = 4
    c = lax.axis_index("ctx")
    t = lax.axis_index("tp")
    chip, core = c // 2, c % 2
    chips = nc // 2
    mate = chip * 2 + 1 - core
    rows = gl_ref.shape[0]
    own = rows // tp
    vocab = gl_ref.shape[1]
    chunks = vocab // chunk
    q_dev = q_ref.shape[0]
    width = gain_ref.shape[1]
    depth = w.shape[0]
    tile = 256

    def remote(src, dst, send, recv, where):
        return pltpu.make_async_remote_copy(
            src_ref=src, dst_ref=dst, send_sem=send, recv_sem=recv, device_id=where, device_id_type=MESH
        )

    def w_copy(j):
        span = pl.ds(pl.multiple_of(j * chunk, chunk), chunk)
        return pltpu.make_async_copy(w_hbm.at[:, span], w.at[:, span], w_sem.at[j])

    wo_copy = pltpu.make_async_copy(wo_hbm, wo, wo_sem)
    wo_copy.start()

    barrier = pltpu.get_barrier_semaphore()
    for d in range(1, nc):
        pl.semaphore_signal(barrier, inc=1, device_id=(lax.rem(c + d, nc), t), device_id_type=MESH)
    for d in range(1, tp):
        pl.semaphore_signal(barrier, inc=1, device_id=(c, lax.rem(t + d, tp)), device_id_type=MESH)
    pl.semaphore_wait(barrier, nc + tp - 2)

    def gather(buf, at, stage):
        def send(idx, d, to):
            return remote(at(buf, idx), at(buf, idx), gather_send.at[stage, d], gather_recv.at[stage, d], (to, t))

        first = [send(c, 0, mate)]
        for d in range(1, chips):
            first.append(send(c, d, lax.rem(chip + d, chips) * 2 + core))
        for copy in first[1:] + first[:1]:
            copy.start()
        passed = []
        for d in range(1, chips):
            first[d].wait_recv()
            idx = lax.rem(chip + chips - d, chips) * 2 + core
            passed.append(send(idx, chips + d, mate))
            passed[-1].start()
        first[0].wait_recv()
        for copy in passed:
            copy.wait_recv()
        for copy in first + passed:
            copy.wait_send()

    tok_dev = k_ref.shape[0]
    kv_all[c, pl.ds(0, tok_dev), :] = k_ref[...]
    kv_all[c, pl.ds(tok_dev, tok_dev), :] = v_ref[...]
    gather(kv_all, lambda buf, idx: buf.at[idx], 0)
    for j in range(chunks):
        w_copy(j).start()

    local_kv = k_ref.shape[1] // HEAD_SIZE
    group = QUERY_HEADS // KEY_VALUE_HEADS
    visible = kpos_ref[...] <= qpos_ref[...]
    pieces = []
    for k in range(local_kv):
        lanes = pl.ds(k * HEAD_SIZE, HEAD_SIZE)
        heads = [
            q_ref[:, (k * group + g) * HEAD_SIZE : (k * group + g + 1) * HEAD_SIZE] for g in range(group)
        ]
        keys = kv_all[:, pl.ds(0, tok_dev), lanes].reshape(nc * tok_dev, HEAD_SIZE)
        values = kv_all[:, pl.ds(tok_dev, tok_dev), lanes].reshape(nc * tok_dev, HEAD_SIZE)
        scores = lax.dot_general(
            jnp.concatenate(heads, axis=0), keys, (((1,), (1,)), ((), ())), preferred_element_type=F32
        ) * HEAD_SIZE ** (-0.5)
        scores = jnp.where(visible, scores, MASKED)
        weights = jnp.exp(scores - jnp.max(scores, axis=1, keepdims=True))
        weights = weights / jnp.sum(weights, axis=1, keepdims=True)
        mixed = jnp.dot(weights.astype(BF16), values, preferred_element_type=F32).astype(BF16)
        for g in range(group):
            pieces.append(mixed[g * q_dev : (g + 1) * q_dev])
    attn[pl.ds(pl.multiple_of(c * q_dev, 16), q_dev), :] = jnp.concatenate(pieces, axis=1)
    gather(attn, lambda buf, idx: buf.at[pl.ds(pl.multiple_of(idx * q_dev, 16), q_dev), :], 1)

    wo_copy.wait()

    def project(owner):
        columns = pl.ds(pl.multiple_of(owner * width, width), width)
        return jnp.dot(attn[...], wo[:, columns], preferred_element_type=F32)

    mixes = []
    for d in range(1, tp):
        owner = lax.rem(t + d, tp)
        mix_out[d - 1] = project(owner).astype(BF16)
        copy = remote(
            mix_out.at[d - 1], mix_in.at[d - 1], mix_sem.at[0, d - 1], mix_sem.at[1, d - 1], (c, owner)
        )
        copy.start()
        mixes.append(copy)
    hidden = resid_ref[...].astype(F32) + project(t)
    for copy in mixes:
        copy.wait()
    for d in range(1, tp):
        hidden = hidden + mix_in[d - 1].astype(F32)

    squares = jnp.sum(hidden * hidden, axis=1, keepdims=True)
    square_tp[0] = jnp.broadcast_to(squares, (rows, rows)).T[0:8]
    copies = []
    for d in range(1, tp):
        copy = remote(
            square_tp.at[0], square_tp.at[d], square_sem.at[0, d], square_sem.at[1, d], (c, lax.rem(t + d, tp))
        )
        copy.start()
        copies.append(copy)
    for copy in copies:
        copy.wait()
    square_ctx[0] = square_tp[0] + square_tp[1] + square_tp[2] + square_tp[3]
    copies = []
    for d in range(1, nc):
        copy = remote(
            square_ctx.at[0], square_ctx.at[d], cross_sem.at[0, d], cross_sem.at[1, d], (lax.rem(c + d, nc), t)
        )
        copy.start()
        copies.append(copy)
    for copy in copies:
        copy.wait()
    total = square_ctx[0]
    for d in range(1, nc):
        total = total + square_ctx[d]
    scale = lax.rsqrt(total / D + EPSILON)
    scale = jnp.broadcast_to(scale[0:1], (rows, rows)).T
    scale = jnp.concatenate([scale] * (width // rows), axis=1)
    norm_all[c] = (hidden * scale * gain_ref[...]).astype(BF16)
    gather(norm_all, lambda buf, idx: buf.at[idx], 2)
    for i in range(nc):
        block_ref[:, i * width : (i + 1) * width] = norm_all[i]

    inner = jnp.logical_or(t == 1, t == 2)
    pair_mate = t + 1 - 2 * (t % 2)
    first_far = 2 - 2 * (t // 2)
    rest = rows - own
    rest_at = jnp.where(t < 2, own, 0)
    far_in_rest = jnp.where(t < 2, own, 0)
    own_in_rest = jnp.where(t < 2, 0, 2 * own)

    def columns_of(j):
        return pl.ds(pl.multiple_of(j * chunk, chunk), chunk)

    def end_copy(j):
        cols = columns_of(j)
        return remote(
            part_out.at[pl.ds(pl.multiple_of(jnp.where(t < 2, own, 0), 16), rest), cols],
            pair_in.at[pl.ds(0, rest), cols],
            part_send.at[0, j],
            part_recv.at[0, j],
            (c, pair_mate),
        )

    def inner_copy(j):
        cols = columns_of(j)
        return remote(
            part_out.at[pl.ds(pl.multiple_of(pair_mate * own, 16), own), cols],
            pair_in.at[pl.ds(0, own), cols],
            part_send.at[0, j],
            part_recv.at[0, j],
            (c, pair_mate),
        )

    def far_copy(j, i):
        cols = columns_of(j)
        owner = first_far + i
        return remote(
            part_out.at[pl.ds(pl.multiple_of(owner * own, 16), own), cols],
            far_in.at[:, cols],
            part_send.at[1 + i, j],
            part_recv.at[1, j],
            (c, owner),
        )

    own_rows = pl.ds(pl.multiple_of(t * own, 16), own)

    @pl.loop(0, chunks)
    def _(j):
        w_copy(j).wait()

        @pl.loop(0, chunk // tile)
        def _(i):
            cols = pl.ds(pl.multiple_of(j * chunk + i * tile, tile), tile)
            hidden_grad[:, 0:tile] = jnp.dot(block_ref[...], w[:, cols], preferred_element_type=F32)
            part_out[:, cols] = hidden_grad[:, 0:tile].astype(BF16)
            logit[:, cols] = hidden_grad[own_rows, 0:tile]

        @pl.when(inner)
        def _():
            inner_copy(j).start()

        @pl.when(jnp.logical_not(inner))
        def _():
            end_copy(j).start()

    @pl.when(inner)
    def _():
        @pl.loop(0, chunks)
        def _(j):
            cols = columns_of(j)
            end_copy(j).wait_recv()
            far = pl.ds(pl.multiple_of(first_far * own, 16), 2 * own)
            total = part_out[far, cols].astype(F32) + pair_in[
                pl.ds(pl.multiple_of(far_in_rest, 16), 2 * own), cols
            ].astype(F32)
            part_out[far, cols] = total.astype(BF16)
            far_copy(j, 0).start()
            far_copy(j, 1).start()
            logit[:, cols] += pair_in[pl.ds(pl.multiple_of(own_in_rest, 16), own), cols].astype(F32)

    first_col = c * vocab
    hits = target_ref[own_rows, :] - first_col

    def column_ids(j):
        return lax.broadcasted_iota(jnp.int32, (own, chunk), 1) + j * chunk

    def settle(j, state):
        peak, sums, picked = state
        cols = columns_of(j)

        @pl.when(jnp.logical_not(inner))
        def _():
            inner_copy(j).wait_recv()
            logit[:, cols] += pair_in[0:own, cols].astype(F32)

        far_copy(j, 0).wait_recv()
        values = logit[:, cols] + far_in[:, cols].astype(F32)
        logit[:, cols] = values
        fresh = jnp.maximum(peak, jnp.max(values, axis=1, keepdims=True))
        sums = sums * jnp.exp(peak - fresh) + jnp.sum(jnp.exp(values - fresh), axis=1, keepdims=True)
        picked = picked + jnp.sum(jnp.where(column_ids(j) == hits, values, 0.0), axis=1, keepdims=True)
        return fresh, sums, picked

    zero = jnp.zeros((own, 1), F32)
    peak, sums, picked = lax.fori_loop(0, chunks, settle, (zero + MASKED, zero, zero))

    lane = lax.broadcasted_iota(jnp.int32, (own, 128), 1)
    pack[...] = jnp.where(lane == 0, peak, jnp.where(lane == 1, sums, picked))
    copies = []
    for d in range(1, nc):
        copy = remote(pack, stat.at[c], stat_sem.at[0, d], stat_sem.at[1, d], (lax.rem(c + d, nc), t))
        copy.start()
        copies.append(copy)
    stat[c] = pack[...]
    for copy in copies:
        copy.wait()
    top = stat[0][:, 0:1]
    for i in range(1, nc):
        top = jnp.maximum(top, stat[i][:, 0:1])
    sums, picked = zero, zero
    for i in range(nc):
        sums = sums + stat[i][:, 1:2] * jnp.exp(stat[i][:, 0:1] - top)
        picked = picked + stat[i][:, 2:3]
    lse = top + jnp.log(sums)

    loss_all[t] = jnp.broadcast_to(jnp.sum(lse - picked, axis=0, keepdims=True), (8, 128))
    losses = []
    for d in range(1, tp):
        copy = remote(
            loss_all.at[t], loss_all.at[t], loss_sem.at[0, d], loss_sem.at[1, d], (c, lax.rem(t + d, tp))
        )
        copy.start()
        losses.append(copy)

    def share(j, source, step):
        place = gl_ref.at[pl.ds(pl.multiple_of(source * own, 16), own), columns_of(j)]
        to = jnp.where(step > 0, jnp.minimum(t + 1, tp - 1), jnp.maximum(t - 1, 0))
        return remote(
            place, place, share_send.at[(step > 0) * tp + source, j], share_recv.at[source, j], (c, to)
        )

    @pl.loop(0, chunks)
    def _(j):
        cols = columns_of(j)
        grads = jnp.exp(logit[:, cols] - lse) - (column_ids(j) == hits).astype(F32)
        gl_ref[own_rows, cols] = grads.astype(BF16)

        @pl.when(t < tp - 1)
        def _():
            share(j, t, 1).start()

        @pl.when(t > 0)
        def _():
            share(j, t, 0).start()

    hidden_grad[...] = jnp.zeros_like(hidden_grad)

    @pl.loop(0, chunks)
    def _(j):
        for far in range(1, tp):

            @pl.when(t - far >= 0)
            def _():
                share(j, t - far, 1).wait_recv()

                @pl.when(t < tp - 1)
                def _():
                    share(j, t - far, 1).start()

            @pl.when(t + far < tp)
            def _():
                share(j, t + far, 0).wait_recv()

                @pl.when(t > 0)
                def _():
                    share(j, t + far, 0).start()

        @pl.loop(0, depth // tile)
        def _(i):
            cols = pl.ds(pl.multiple_of(i * tile, tile), tile)
            hidden_grad[:, cols] += lax.dot_general(
                gl_ref[:, columns_of(j)],
                w[cols, columns_of(j)],
                (((1,), (1,)), ((), ())),
                preferred_element_type=F32,
            )

    grad_out[...] = hidden_grad[...].astype(BF16)
    copies = []
    for d in range(1, nc):
        to = lax.rem(c + d, nc)
        copy = remote(
            grad_out.at[pl.ds(pl.multiple_of(to * q_dev, 16), q_dev), :],
            grad_in.at[d - 1],
            grad_sem.at[0, d],
            grad_sem.at[1, d],
            (to, t),
        )
        copy.start()
        copies.append(copy)

    @pl.loop(0, chunks)
    def _(j):
        @pl.when(inner)
        def _():
            inner_copy(j).wait_send()
            far_copy(j, 0).wait_send()
            far_copy(j, 1).wait_send()

        @pl.when(jnp.logical_not(inner))
        def _():
            end_copy(j).wait_send()

        @pl.when(t < tp - 1)
        def _():
            share(j, t, 1).wait_send()
            for far in range(1, tp):

                @pl.when(t - far >= 0)
                def _():
                    share(j, t - far, 1).wait_send()

        @pl.when(t > 0)
        def _():
            share(j, t, 0).wait_send()
            for far in range(1, tp):

                @pl.when(t + far < tp)
                def _():
                    share(j, t + far, 0).wait_send()

    for copy in losses:
        copy.wait()
    loss_ref[...] = (loss_all[0] + loss_all[1] + loss_all[2] + loss_all[3]) / rows

    result = hidden_grad[pl.ds(pl.multiple_of(c * q_dev, 16), q_dev), :]
    for copy in copies:
        copy.wait()
    for d in range(1, nc):
        result = result + grad_in[d - 1].astype(F32)
    gn_ref[...] = result.astype(BF16)


def fused_per_device(
    queries,
    rotated_keys,
    value_rows,
    span_order,
    targets,
    out_weight,
    residual,
    norm_gain,
    head_weight,
):
    nc, tp = lax.axis_size("ctx"), lax.axis_size("tp")
    tok_dev, kv_width = rotated_keys.shape
    q_dev, q_width = queries.shape
    span_rows, q_span = tok_dev // 2, q_dev // 2
    rows = q_dev * nc
    own = rows // tp
    slice_width = out_weight.shape[3]
    depth, vocab = head_weight.shape
    chunk = min(1024, vocab)
    chunks = vocab // chunk
    kpos = slot_positions(span_order, tok_dev * nc, span_rows, span_rows, 0)
    qpos = slot_positions(span_order, rows, q_span, span_rows, span_rows - q_span)
    mine = lax.dynamic_slice_in_dim(qpos, lax.axis_index("ctx") * q_dev, q_dev)
    mine = jnp.tile(mine, QUERY_HEADS // KEY_VALUE_HEADS)[:, None]
    vmem = pl.BlockSpec(memory_space=pltpu.VMEM)
    hbm = pl.BlockSpec(memory_space=pl.ANY)
    dma = pltpu.SemaphoreType.DMA
    loss, grad_normed, block, grad_logits = pl.pallas_call(
        functools.partial(fused_kernel, nc, chunk),
        out_shape=(
            jax.ShapeDtypeStruct((8, 128), F32),
            jax.ShapeDtypeStruct((q_dev, depth), BF16),
            jax.ShapeDtypeStruct((rows, depth), BF16),
            jax.ShapeDtypeStruct((rows, vocab), BF16),
        ),
        in_specs=[vmem] * 6 + [hbm, vmem, vmem, hbm],
        out_specs=(vmem,) * 4,
        scratch_shapes=[
            pltpu.VMEM((depth, vocab), BF16),
            pltpu.VMEM((q_width, tp * slice_width), BF16),
            pltpu.VMEM((nc, 2 * tok_dev, kv_width), BF16),
            pltpu.VMEM((rows, q_width), BF16),
            pltpu.VMEM((tp - 1, rows, slice_width), BF16),
            pltpu.VMEM((tp - 1, rows, slice_width), BF16),
            pltpu.VMEM((tp, 8, rows), F32),
            pltpu.VMEM((nc, 8, rows), F32),
            pltpu.VMEM((nc, rows, slice_width), BF16),
            pltpu.VMEM((rows, vocab), BF16),
            pltpu.VMEM((rows - own, vocab), BF16),
            pltpu.VMEM((own, vocab), BF16),
            pltpu.VMEM((own, vocab), F32),
            pltpu.VMEM((own, 128), F32),
            pltpu.VMEM((nc, own, 128), F32),
            pltpu.VMEM((tp, 8, 128), F32),
            pltpu.VMEM((rows, depth), F32),
            pltpu.VMEM((rows, depth), BF16),
            pltpu.VMEM((nc - 1, q_dev, depth), BF16),
            dma((chunks,)),
            dma,
            dma((3, nc)),
            dma((3, nc)),
            dma((2, tp - 1)),
            dma((2, tp)),
            dma((2, nc)),
            dma((3, chunks)),
            dma((2, chunks)),
            dma((2, nc)),
            dma((2, tp)),
            dma((2 * tp, chunks)),
            dma((tp, chunks)),
            dma((2, nc)),
        ],
        compiler_params=pltpu.CompilerParams(
            collective_id=0, has_side_effects=True, vmem_limit_bytes=58 * 1024 * 1024
        ),
    )(
        queries,
        rotated_keys,
        value_rows,
        kpos[None, :],
        mine,
        targets[:, None],
        out_weight.reshape(q_width, -1),
        residual.reshape(rows, slice_width),
        norm_gain.reshape(1, slice_width),
        head_weight,
    )
    grad_head = lax.dot_general(
        block, grad_logits, (((0,), (0,)), ((), ())), preferred_element_type=jnp.float32
    ).astype(jnp.bfloat16)
    return (loss[0, 0], grad_normed, grad_head)


def fits_kernel(mesh):
    nc, tp = mesh.shape["ctx"], mesh.shape["tp"]
    width = D // (nc * tp)
    return tp == 4 and nc % 2 == 0 and width % 128 == 0


def solution(mesh):
    placed = (
        P("ctx", "tp"),
        P("ctx", "tp"),
        P("ctx", "tp"),
        P(),
        P(),
        P("tp", None, "ctx", None),
        P(None, "tp", "ctx", None),
        P("tp", "ctx", None),
        P("tp", "ctx"),
    )
    return jax.shard_map(
        fused_per_device if fits_kernel(mesh) else per_device,
        mesh=mesh,
        in_specs=placed,
        out_specs=(P(), P("ctx", "tp"), P("tp", "ctx")),
        check_vma=False,
    )
```

```python
import functools

import jax
import jax.numpy as jnp
from jax import lax
from jax.experimental import pallas as pl
from jax.experimental.pallas import tpu as pltpu
from jax.sharding import PartitionSpec as P

D = 8192
QUERY_HEADS = 64
KEY_VALUE_HEADS = 8
HEAD_SIZE = 128


EPSILON = 1e-05
MASKED = -1e30


def slot_positions(span_order, total_rows, slot_rows, span_rows, first_row):
    slots = jnp.arange(total_rows, dtype=jnp.int32)
    owners = slots // slot_rows
    table = owners[:, None] == jnp.arange(span_order.shape[0], dtype=jnp.int32)[None, :]
    starts = jnp.sum(jnp.where(table, span_order[None, :], 0), axis=1)
    return starts * span_rows + first_row + slots % slot_rows


def head_scores(grouped_queries, piece_keys):
    divided_keys = piece_keys.reshape(piece_keys.shape[0], -1, HEAD_SIZE)
    return jnp.einsum(
        "tkgd,skd->kgts", grouped_queries, divided_keys, preferred_element_type=jnp.float32
    ) * HEAD_SIZE ** (-0.5)


def score_stats(grouped_queries, mine, positions):

    def score_update(carry, piece, offset):
        visible = positions[None, :] <= mine[:, None]

        def score_accumulate(state):
            scores = jnp.where(visible, head_scores(grouped_queries, piece), MASKED)
            fresh = jnp.maximum(state[0], jnp.max(scores, axis=-1))
            added = jnp.sum(jnp.where(visible, jnp.exp(scores - fresh[..., None]), 0.0), axis=-1)
            return (fresh, added)

        return lax.cond(jnp.any(visible), score_accumulate, lambda state: state, carry)

    return score_update


def weighted_values(grouped_queries, mine, positions, peak, totals):

    def weighted_update(carry, pieces, offset):
        piece_keys, piece_values = pieces
        visible = positions[None, :] <= mine[:, None]

        def weighted_accumulate(state):
            scores = jnp.where(visible, head_scores(grouped_queries, piece_keys), MASKED)
            weights = jnp.where(visible, jnp.exp(scores - peak[..., None]), 0.0) / totals[..., None]
            divided_values = piece_values.reshape(piece_values.shape[0], -1, HEAD_SIZE)
            return jnp.einsum(
                "kgts,skd->tkgd",
                weights.astype(jnp.bfloat16),
                divided_values,
                preferred_element_type=jnp.float32,
            )

        return lax.cond(jnp.any(visible), weighted_accumulate, lambda state: state, carry)

    return weighted_update


def per_device(
    queries,
    rotated_keys,
    value_rows,
    span_order,
    targets,
    out_weight,
    residual,
    norm_gain,
    head_weight,
):
    tok_dev = rotated_keys.shape[0]
    q_dev = queries.shape[0]
    span_rows = tok_dev // 2
    q_span = q_dev // 2
    total_keys = tok_dev * lax.axis_size("ctx")
    total_rows = q_dev * lax.axis_size("ctx")
    positions = slot_positions(span_order, total_keys, span_rows, span_rows, 0)
    query_pos = slot_positions(span_order, total_rows, q_span, span_rows, span_rows - q_span)
    mine = lax.dynamic_slice_in_dim(query_pos, lax.axis_index("ctx") * q_dev, q_dev)
    group_size = QUERY_HEADS // KEY_VALUE_HEADS
    local_kv = rotated_keys.shape[1] // HEAD_SIZE
    grouped_queries = queries.reshape(q_dev, local_kv, group_size, HEAD_SIZE)
    start_stats = (
        jnp.full((local_kv, group_size, q_dev), MASKED, jnp.float32),
        jnp.zeros((local_kv, group_size, q_dev), jnp.float32),
    )
    start_acc = jnp.zeros((q_dev, local_kv, group_size, HEAD_SIZE), jnp.float32)
    stats_step = score_stats(grouped_queries, mine, positions)
    all_keys, all_values = (
        lax.all_gather(rotated_keys, "ctx", axis=0, tiled=True),
        lax.all_gather(value_rows, "ctx", axis=0, tiled=True),
    )
    peak, totals = stats_step(start_stats, all_keys, 0)
    value_step = weighted_values(grouped_queries, mine, positions, peak, totals)
    attn_acc = value_step(start_acc, (all_keys, all_values), 0)
    attn = attn_acc.astype(jnp.bfloat16).reshape(q_dev, -1)
    slice_width = out_weight.shape[3]
    out_local = out_weight.reshape(out_weight.shape[0], -1)
    mixed = jnp.dot(
        lax.all_gather(attn, "ctx", axis=0, tiled=True),
        out_local,
        preferred_element_type=jnp.float32,
    )
    mixed = lax.psum_scatter(
        mixed.reshape(total_rows, -1, slice_width), "tp", scatter_dimension=1, tiled=True
    )
    hidden = residual.reshape(total_rows, slice_width).astype(jnp.float32) + mixed.reshape(
        total_rows, slice_width
    )
    squares = lax.psum(jnp.sum(hidden * hidden, axis=1), ("ctx", "tp"))
    normed = (
        hidden * lax.rsqrt(squares / D + EPSILON)[:, None] * norm_gain.reshape(1, slice_width)
    ).astype(jnp.bfloat16)
    block = lax.all_gather(normed, "ctx", axis=1, tiled=True)
    vocab_width = head_weight.shape[1]
    first_col = lax.axis_index("ctx") * vocab_width
    logits = lax.psum_scatter(
        jnp.dot(block, head_weight, preferred_element_type=jnp.float32),
        "tp",
        scatter_dimension=0,
        tiled=True,
    )
    row_targets = lax.dynamic_slice_in_dim(
        targets, lax.axis_index("tp") * logits.shape[0], logits.shape[0]
    )
    columns = jnp.arange(vocab_width, dtype=jnp.int32)[None, :] + first_col
    target_hit = columns == row_targets[:, None]
    local_peak = jnp.max(logits, axis=1)
    picked = jnp.sum(jnp.where(target_hit, logits, 0.0), axis=1)
    row_peak = lax.pmax(local_peak, "ctx")
    expsum = jnp.sum(jnp.exp(logits - row_peak[:, None]), axis=1)
    expsum, picked = lax.psum((expsum, picked), "ctx")
    lse = row_peak + jnp.log(expsum)
    grad_logits = (jnp.exp(logits - lse[:, None]) - target_hit.astype(jnp.float32)).astype(
        jnp.bfloat16
    )
    loss_part = jnp.sum(lse - picked)
    loss = lax.psum(loss_part, "tp") / total_rows
    grad_logits = lax.all_gather(grad_logits, "tp", axis=0, tiled=True)
    grad_normed = lax.psum_scatter(
        lax.dot_general(
            grad_logits, head_weight, (((1,), (1,)), ((), ())), preferred_element_type=jnp.float32
        ),
        "ctx",
        scatter_dimension=0,
        tiled=True,
    ).astype(jnp.bfloat16)
    grad_head = lax.dot_general(
        block, grad_logits, (((0,), (0,)), ((), ())), preferred_element_type=jnp.float32
    ).astype(jnp.bfloat16)
    return (loss, grad_normed, grad_head)


MESH = pl.DeviceIdType.MESH
F32 = jnp.float32
BF16 = jnp.bfloat16
PART = jnp.int16
PART_TOP = 32767.0


def fused_kernel(
    nc,
    chunk,
    q_ref,
    k_ref,
    v_ref,
    span_ref,
    target_ref,
    wo_hbm,
    resid_ref,
    gain_ref,
    w_hbm,
    loss_ref,
    gn_ref,
    block_ref,
    gl_ref,
    w,
    wo,
    kv_all,
    attn,
    mix_out,
    mix_in,
    square_tp,
    square_ctx,
    norm_all,
    block,
    scales,
    part_out,
    right_in,
    left_in,
    step_out,
    step_in,
    logit,
    pack,
    stat,
    loss_all,
    hidden_grad,
    hidden_back,
    grad_out,
    grad_in,
    w_sem,
    wo_sem,
    gather_send,
    gather_recv,
    mix_sem,
    square_sem,
    cross_sem,
    part_send,
    part_recv,
    step_send,
    step_recv,
    stat_sem,
    loss_sem,
    share_send,
    share_recv,
    grad_sem,
):
    tp = 4
    c = lax.axis_index("ctx")
    t = lax.axis_index("tp")
    chip, core = c // 2, c % 2
    chips = nc // 2
    mate = chip * 2 + 1 - core
    rows = gl_ref.shape[0]
    own = rows // 2
    vocab = gl_ref.shape[1]
    chunks = vocab // chunk
    q_dev = q_ref.shape[0]
    width = gain_ref.shape[1]
    depth = w.shape[0]
    tile = 256
    back = min(1024, depth)

    def remote(src, dst, send, recv, where):
        return pltpu.make_async_remote_copy(
            src_ref=src, dst_ref=dst, send_sem=send, recv_sem=recv, device_id=where, device_id_type=MESH
        )

    def w_copy(j):
        span = pl.ds(pl.multiple_of(j * chunk, chunk), chunk)
        return pltpu.make_async_copy(w_hbm.at[:, span], w.at[:, span], w_sem.at[j])

    wo_copy = pltpu.make_async_copy(wo_hbm, wo, wo_sem)
    wo_copy.start()

    barrier = pltpu.get_barrier_semaphore()
    for d in range(1, nc):
        pl.semaphore_signal(barrier, inc=1, device_id=(lax.rem(c + d, nc), t), device_id_type=MESH)
    for d in range(1, tp):
        pl.semaphore_signal(barrier, inc=1, device_id=(c, lax.rem(t + d, tp)), device_id_type=MESH)
    pl.semaphore_wait(barrier, nc + tp - 2)

    def gather(buf, at, stage):
        def send(idx, d, to):
            return remote(at(buf, idx), at(buf, idx), gather_send.at[stage, d], gather_recv.at[stage, d], (to, t))

        first = [send(c, 0, mate)]
        for d in range(1, chips):
            first.append(send(c, d, lax.rem(chip + d, chips) * 2 + core))
        for copy in first[1:] + first[:1]:
            copy.start()
        passed = []
        for d in range(1, chips):
            first[d].wait_recv()
            idx = lax.rem(chip + chips - d, chips) * 2 + core
            passed.append(send(idx, chips + d, mate))
            passed[-1].start()
        first[0].wait_recv()
        for copy in passed:
            copy.wait_recv()
        for copy in first + passed:
            copy.wait_send()

    tok_dev = k_ref.shape[0]
    kv_all[c, pl.ds(0, tok_dev), :] = k_ref[...]
    kv_all[c, pl.ds(tok_dev, tok_dev), :] = v_ref[...]
    gather(kv_all, lambda buf, idx: buf.at[idx], 0)
    for j in range(chunks):
        w_copy(j).start()

    local_kv = k_ref.shape[1] // HEAD_SIZE
    group = QUERY_HEADS // KEY_VALUE_HEADS
    span_rows, q_span = tok_dev // 2, q_dev // 2
    lanes = lax.broadcasted_iota(jnp.int32, (group * q_dev, nc * tok_dev), 1)
    kpos = lanes
    for i in range(2 * nc):
        inside = jnp.logical_and(lanes >= i * span_rows, lanes < (i + 1) * span_rows)
        kpos = jnp.where(inside, lanes + (span_ref[i] - i) * span_rows, kpos)
    lines = lax.broadcasted_iota(jnp.int32, (group * q_dev, nc * tok_dev), 0)
    qpos = lines
    for i in range(2 * group):
        inside = jnp.logical_and(lines >= i * q_span, lines < (i + 1) * q_span)
        start = (span_ref[2 * c + i % 2] + 1) * span_rows - q_span - i * q_span
        qpos = jnp.where(inside, lines + start, qpos)
    visible = kpos <= qpos
    pieces = []
    for k in range(local_kv):
        lanes = pl.ds(k * HEAD_SIZE, HEAD_SIZE)
        heads = [
            q_ref[:, (k * group + g) * HEAD_SIZE : (k * group + g + 1) * HEAD_SIZE] for g in range(group)
        ]
        keys = kv_all[:, pl.ds(0, tok_dev), lanes].reshape(nc * tok_dev, HEAD_SIZE)
        values = kv_all[:, pl.ds(tok_dev, tok_dev), lanes].reshape(nc * tok_dev, HEAD_SIZE)
        scores = lax.dot_general(
            jnp.concatenate(heads, axis=0), keys, (((1,), (1,)), ((), ())), preferred_element_type=F32
        ) * HEAD_SIZE ** (-0.5)
        scores = jnp.where(visible, scores, MASKED)
        weights = jnp.exp(scores - jnp.max(scores, axis=1, keepdims=True))
        weights = weights / jnp.sum(weights, axis=1, keepdims=True)
        mixed = jnp.dot(weights.astype(BF16), values, preferred_element_type=F32).astype(BF16)
        for g in range(group):
            pieces.append(mixed[g * q_dev : (g + 1) * q_dev])
    attn[pl.ds(pl.multiple_of(c * q_dev, 16), q_dev), :] = jnp.concatenate(pieces, axis=1)
    gather(attn, lambda buf, idx: buf.at[pl.ds(pl.multiple_of(idx * q_dev, 16), q_dev), :], 1)

    wo_copy.wait()

    def project(owner):
        columns = pl.ds(pl.multiple_of(owner * width, width), width)
        return jnp.dot(attn[...], wo[:, columns], preferred_element_type=F32)

    mixes = []
    for d in range(1, tp):
        owner = lax.rem(t + d, tp)
        mix_out[d - 1] = project(owner).astype(BF16)
        copy = remote(
            mix_out.at[d - 1], mix_in.at[d - 1], mix_sem.at[0, d - 1], mix_sem.at[1, d - 1], (c, owner)
        )
        copy.start()
        mixes.append(copy)
    hidden = resid_ref[...].astype(F32) + project(t)
    for copy in mixes:
        copy.wait()
    for d in range(1, tp):
        hidden = hidden + mix_in[d - 1].astype(F32)

    squares = jnp.sum(hidden * hidden, axis=1, keepdims=True)
    square_tp[0] = jnp.broadcast_to(squares, (rows, rows)).T[0:8]
    copies = []
    for d in range(1, tp):
        copy = remote(
            square_tp.at[0], square_tp.at[d], square_sem.at[0, d], square_sem.at[1, d], (c, lax.rem(t + d, tp))
        )
        copy.start()
        copies.append(copy)
    for copy in copies:
        copy.wait()
    square_ctx[0] = square_tp[0] + square_tp[1] + square_tp[2] + square_tp[3]
    copies = []
    for d in range(1, nc):
        copy = remote(
            square_ctx.at[0], square_ctx.at[d], cross_sem.at[0, d], cross_sem.at[1, d], (lax.rem(c + d, nc), t)
        )
        copy.start()
        copies.append(copy)
    for copy in copies:
        copy.wait()
    total = square_ctx[0]
    for d in range(1, nc):
        total = total + square_ctx[d]
    scale = lax.rsqrt(total / D + EPSILON)
    scale = jnp.broadcast_to(scale[0:1], (rows, rows)).T
    scale = jnp.concatenate([scale] * (width // rows), axis=1)
    norm_all[c] = (hidden * scale * gain_ref[...]).astype(BF16)
    gather(norm_all, lambda buf, idx: buf.at[idx], 2)
    for i in range(nc):
        block[:, i * width : (i + 1) * width] = norm_all[i]

    last = tp - 1
    end = jnp.logical_or(t == 0, t == last)
    middle = jnp.logical_not(end)
    side = t // 2
    low, high = pl.ds(0, own), pl.ds(own, own)
    own_rows = pl.ds(pl.multiple_of(side * own, 16), own)

    def columns_of(j):
        return pl.ds(pl.multiple_of(j * chunk, chunk), chunk)

    def right_sum(j):
        return remote(
            part_out.at[low, columns_of(j)],
            right_in.at[:, columns_of(j)],
            part_send.at[0, j],
            part_recv.at[0, j],
            (c, jnp.minimum(t + 1, last)),
        )

    def left_sum(j):
        return remote(
            part_out.at[high, columns_of(j)],
            left_in.at[:, columns_of(j)],
            part_send.at[1, j],
            part_recv.at[1, j],
            (c, jnp.maximum(t - 1, 0)),
        )

    def step_copy(j, way):
        to = jnp.minimum(t + 1, last) if way == 0 else jnp.maximum(t - 1, 0)
        return remote(step_out.at[way, j], step_in.at[way, j], step_send.at[way, j], step_recv.at[way, j], (c, to))

    def encode(j, way, values):
        top = jnp.max(jnp.max(jnp.abs(values), axis=1, keepdims=True), axis=0, keepdims=True)
        top = jnp.maximum(top, 1e-20)
        coded = jnp.floor(values * (PART_TOP / top) + 0.5).astype(jnp.int32).astype(PART)
        part_out[low if way == 0 else high, columns_of(j)] = coded
        step_out[way, j] = jnp.broadcast_to(top / PART_TOP, (8, 128))
        step_copy(j, way).start()
        (right_sum if way == 0 else left_sum)(j).start()

    def arrived(j, way):
        step_copy(j, way).wait_recv()
        (right_sum if way == 0 else left_sum)(j).wait_recv()
        coded = (right_in if way == 0 else left_in)[:, columns_of(j)]
        return coded.astype(jnp.int32).astype(F32) * step_in[way, j][0:1, 0:1]

    def combine(j, way, place):
        @pl.when(jnp.logical_and(middle, jnp.logical_and(j >= 0, j < chunks)))
        def _():
            k = jnp.clip(j, 0, chunks - 1)
            encode(k, way, logit[place, columns_of(k)] + arrived(k, way))

    lag = 2

    @pl.loop(0, chunks + lag * (tp - 2))
    def _(step):
        @pl.when(step < chunks)
        def _():
            w_copy(step).wait()

            @pl.loop(0, chunk // tile)
            def _(i):
                cols = pl.ds(pl.multiple_of(step * chunk + i * tile, tile), tile)
                logit[:, cols] = jnp.dot(block[...], w[:, cols], preferred_element_type=F32)

            @pl.when(t == 0)
            def _():
                encode(step, 0, logit[high, columns_of(step)])

            @pl.when(t == last)
            def _():
                encode(step, 1, logit[low, columns_of(step)])

        combine(step - lag * t, 0, high)
        combine(step - lag * (last - t), 1, low)

    for i in range(depth // rows):
        columns = slice(i * rows, (i + 1) * rows)
        block_ref[columns, :] = block[:, columns].astype(F32).T.astype(BF16)

    scales[...] = jnp.broadcast_to(target_ref[...].astype(F32), (rows, rows)).T
    first_col = c * vocab
    hits = scales[own_rows, 0:1].astype(jnp.int32) - first_col

    def column_ids(j):
        return lax.broadcasted_iota(jnp.int32, (own, chunk), 1) + j * chunk

    def loss_copy(d):
        return remote(
            loss_all.at[side], loss_all.at[side], loss_sem.at[0, d], loss_sem.at[1, side], (c, lax.rem(t + d, tp))
        )

    def stat_copy(d):
        return remote(pack, stat.at[c], stat_sem.at[0, d], stat_sem.at[1, d], (lax.rem(c + d, nc), t))

    def settle(j, state):
        peak, sums, picked = state
        cols = columns_of(j)

        @pl.when(t == 0)
        def _():
            logit[low, cols] += arrived(j, 1)

        @pl.when(t == last)
        def _():
            logit[high, cols] += arrived(j, 0)

        values = logit[own_rows, cols]
        fresh = jnp.maximum(peak, jnp.max(values, axis=1, keepdims=True))
        sums = sums * jnp.exp(peak - fresh) + jnp.sum(jnp.exp(values - fresh), axis=1, keepdims=True)
        picked = picked + jnp.sum(jnp.where(column_ids(j) == hits, values, 0.0), axis=1, keepdims=True)
        return fresh, sums, picked

    @pl.when(end)
    def _():
        zero = jnp.zeros((own, 1), F32)
        peak, sums, picked = lax.fori_loop(0, chunks, settle, (zero + MASKED, zero, zero))
        lane = lax.broadcasted_iota(jnp.int32, (own, 128), 1)
        pack[...] = jnp.where(lane == 0, peak, jnp.where(lane == 1, sums, picked))
        for d in range(1, nc):
            stat_copy(d).start()
        stat[c] = pack[...]
        for d in range(1, nc):
            stat_copy(d).wait()
        top = stat[0][:, 0:1]
        for i in range(1, nc):
            top = jnp.maximum(top, stat[i][:, 0:1])
        sums, picked = zero, zero
        for i in range(nc):
            sums = sums + stat[i][:, 1:2] * jnp.exp(stat[i][:, 0:1] - top)
            picked = picked + stat[i][:, 2:3]
        lse = top + jnp.log(sums)
        loss_all[side] = jnp.broadcast_to(jnp.sum(lse - picked, axis=0, keepdims=True), (8, 128))
        for d in range(1, tp):
            loss_copy(d).start()
        pack[...] = jnp.broadcast_to(lse, (own, 128))

    def share(j, place, to, way):
        cell = gl_ref.at[place, columns_of(j)]
        return remote(cell, cell, share_send.at[way, j], share_recv.at[way, j], (c, to))

    def right_share(j):
        return share(j, low, jnp.minimum(t + 1, last), 0)

    def left_share(j):
        return share(j, high, jnp.maximum(t - 1, 0), 1)

    hidden_back[...] = jnp.zeros_like(hidden_back)

    def settled(j):
        @pl.loop(0, depth // back)
        def _(i):
            lines = pl.ds(pl.multiple_of(i * back, back), back)
            hidden_back[lines, :] += lax.dot_general(
                w[lines, columns_of(j)],
                gl_ref[:, columns_of(j)],
                (((1,), (1,)), ((), ())),
                preferred_element_type=F32,
            )

    def relay(j, copy, sends, arrives):
        live = jnp.logical_and(j >= 0, j < chunks)
        k = jnp.clip(j, 0, chunks - 1)

        @pl.when(jnp.logical_and(live, arrives))
        def _():
            copy(k).wait_recv()

        @pl.when(jnp.logical_and(live, sends))
        def _():
            copy(k).start()

    @pl.loop(0, chunks + last)
    def _(step):
        @pl.when(jnp.logical_and(end, step < chunks))
        def _():
            cols = columns_of(jnp.minimum(step, chunks - 1))
            grads = jnp.exp(logit[own_rows, cols] - pack[:, 0:1])
            grads = grads - (column_ids(step) == hits).astype(F32)
            gl_ref[own_rows, cols] = grads.astype(BF16)

        relay(step - t, right_share, t < last, t > 0)
        relay(step - (last - t), left_share, t > 0, t < last)

        @pl.when(step >= last)
        def _():
            settled(step - last)

    for i in range(depth // rows):
        columns = slice(i * rows, (i + 1) * rows)
        hidden_grad[:, columns] = hidden_back[columns, :].T
    grad_out[...] = hidden_grad[...].astype(BF16)
    copies = []
    for d in range(1, nc):
        to = lax.rem(c + d, nc)
        copy = remote(
            grad_out.at[pl.ds(pl.multiple_of(to * q_dev, 16), q_dev), :],
            grad_in.at[d - 1],
            grad_sem.at[0, d],
            grad_sem.at[1, d],
            (to, t),
        )
        copy.start()
        copies.append(copy)

    @pl.loop(0, chunks)
    def _(j):
        @pl.when(t < last)
        def _():
            step_copy(j, 0).wait_send()
            right_sum(j).wait_send()
            right_share(j).wait_send()

        @pl.when(t > 0)
        def _():
            step_copy(j, 1).wait_send()
            left_sum(j).wait_send()
            left_share(j).wait_send()

    def loss_wait(i):
        return remote(loss_all.at[i], loss_all.at[i], loss_sem.at[0, 0], loss_sem.at[1, i], (c, lax.rem(t + 1, tp)))

    @pl.when(end)
    def _():
        for d in range(1, tp):
            loss_copy(d).wait_send()

    @pl.when(t != 0)
    def _():
        loss_wait(0).wait_recv()

    @pl.when(t != last)
    def _():
        loss_wait(1).wait_recv()

    losses_sum = loss_all[0] + loss_all[1]
    loss_ref[...] = losses_sum[0:1, 0:1] / rows

    result = hidden_grad[pl.ds(pl.multiple_of(c * q_dev, 16), q_dev), :]
    for copy in copies:
        copy.wait()
    for d in range(1, nc):
        result = result + grad_in[d - 1].astype(F32)
    gn_ref[...] = result.astype(BF16)


def fused_per_device(
    queries,
    rotated_keys,
    value_rows,
    span_order,
    targets,
    out_weight,
    residual,
    norm_gain,
    head_weight,
):
    nc, tp = lax.axis_size("ctx"), lax.axis_size("tp")
    tok_dev, kv_width = rotated_keys.shape
    q_dev, q_width = queries.shape
    rows = q_dev * nc
    own = rows // 2
    slice_width = out_weight.shape[3]
    depth, vocab = head_weight.shape
    chunk = min(512, vocab)
    chunks = vocab // chunk
    vmem = pl.BlockSpec(memory_space=pltpu.VMEM)
    hbm = pl.BlockSpec(memory_space=pl.ANY)
    dma = pltpu.SemaphoreType.DMA
    loss, grad_normed, block, grad_logits = pl.pallas_call(
        functools.partial(fused_kernel, nc, chunk),
        out_shape=(
            jax.ShapeDtypeStruct((1, 1), F32),
            jax.ShapeDtypeStruct((q_dev, depth), BF16),
            jax.ShapeDtypeStruct((depth, rows), BF16),
            jax.ShapeDtypeStruct((rows, vocab), BF16),
        ),
        in_specs=[vmem] * 3 + [pl.BlockSpec(memory_space=pltpu.SMEM), vmem, hbm, vmem, vmem, hbm],
        out_specs=(vmem,) * 4,
        scratch_shapes=[
            pltpu.VMEM((depth, vocab), BF16),
            pltpu.VMEM((q_width, tp * slice_width), BF16),
            pltpu.VMEM((nc, 2 * tok_dev, kv_width), BF16),
            pltpu.VMEM((rows, q_width), BF16),
            pltpu.VMEM((tp - 1, rows, slice_width), BF16),
            pltpu.VMEM((tp - 1, rows, slice_width), BF16),
            pltpu.VMEM((tp, 8, rows), F32),
            pltpu.VMEM((nc, 8, rows), F32),
            pltpu.VMEM((nc, rows, slice_width), BF16),
            pltpu.VMEM((rows, depth), BF16),
            pltpu.VMEM((rows, rows), F32),
            pltpu.VMEM((rows, vocab), PART),
            pltpu.VMEM((own, vocab), PART),
            pltpu.VMEM((own, vocab), PART),
            pltpu.VMEM((2, chunks, 8, 128), F32),
            pltpu.VMEM((2, chunks, 8, 128), F32),
            pltpu.VMEM((rows, vocab), F32),
            pltpu.VMEM((own, 128), F32),
            pltpu.VMEM((nc, own, 128), F32),
            pltpu.VMEM((2, 8, 128), F32),
            pltpu.VMEM((rows, depth), F32),
            pltpu.VMEM((depth, rows), F32),
            pltpu.VMEM((rows, depth), BF16),
            pltpu.VMEM((nc - 1, q_dev, depth), BF16),
            dma((chunks,)),
            dma,
            dma((3, nc)),
            dma((3, nc)),
            dma((2, tp - 1)),
            dma((2, tp)),
            dma((2, nc)),
            dma((2, chunks)),
            dma((2, chunks)),
            dma((2, chunks)),
            dma((2, chunks)),
            dma((2, nc)),
            dma((2, tp)),
            dma((2, chunks)),
            dma((2, chunks)),
            dma((2, nc)),
        ],
        compiler_params=pltpu.CompilerParams(
            collective_id=0, has_side_effects=True, vmem_limit_bytes=58 * 1024 * 1024
        ),
    )(
        queries,
        rotated_keys,
        value_rows,
        span_order,
        targets[None, :],
        out_weight.reshape(q_width, -1),
        residual.reshape(rows, slice_width),
        norm_gain.reshape(1, slice_width),
        head_weight,
    )
    grad_head = jnp.dot(block, grad_logits, preferred_element_type=F32).astype(BF16)
    return (loss[0, 0], grad_normed, grad_head)


def fits_kernel(mesh):
    nc, tp = mesh.shape["ctx"], mesh.shape["tp"]
    width = D // (nc * tp)
    return tp == 4 and nc % 2 == 0 and width % 128 == 0


def solution(mesh):
    placed = (
        P("ctx", "tp"),
        P("ctx", "tp"),
        P("ctx", "tp"),
        P(),
        P(),
        P("tp", None, "ctx", None),
        P(None, "tp", "ctx", None),
        P("tp", "ctx", None),
        P("tp", "ctx"),
    )
    return jax.shard_map(
        fused_per_device if fits_kernel(mesh) else per_device,
        mesh=mesh,
        in_specs=placed,
        out_specs=(P(), P("ctx", "tp"), P("tp", "ctx")),
        check_vma=False,
    )
```
